256 devices in a mesh: section: 32 (over x, z_lo, core), sp: 8 (over z_hi, y).
Axes of the slice: x: 4, y: 4, z: 8 (z_hi: 2, z_lo: 4; z = z_hi * 4 + z_lo), core: 2. Of those that a mesh axis runs over, the one named last changes fastest.
Arguments:
- segment_starting_activations: bfloat16 [32, 256, 2560], P('section', 'sp'), may hold values from -40 to 40
- prior_step_memory_pairs: bfloat16 [32, 2, 768, 3072], P('section', None, None, 'sp'), may hold values from -3 to 3
- triple_projection_matrix: bfloat16 [32, 2560, 3, 3072], P('section', None, None, 'sp'), may hold values from -0.125 to 0.125
- final_projection_matrix: bfloat16 [32, 3072, 2560], P('section', 'sp'), may hold values from -0.109375 to 0.109375
- layer_gain_factors: float32 [32, 2560], P('section'), may hold values from 0.5 to 2
- tile_element_counts: int32 [4], replicated, may hold values from 1 to 256, 768 in all
- tile_visit_order: int32 [4], replicated, may hold values from 0 to 3, each once
Outputs:
- outflight: bfloat16 [32, 256, 2560], P('section', 'sp')
- new_cache: bfloat16 [32, 2, 768, 3072], P('section', None, None, 'sp')
The draws below stay inside these ranges and needn't reach their ends.
Inputs may be any that keep to these rules, and one draw needn't show every extreme that they name: `tile_element_counts`: the patches cover the 768 tokens of the clip in order; the entries sum to 768 and the largest is 256. `tile_visit_order`: each patch appears once.
All inputs are finite; a program needn't handle non-finite values.
Results may differ from the reference program's by a relative error of at most 0.022.
Values may be sent and summed in bfloat16 or wider, within the bound.
A program may use at most 64 MiB of HBM per device.

```python
import math
import jax
import jax.numpy as jnp
import numpy as np
from jax import lax

D = 2560
HEADS = 24
HD = 128
INNER = 3072
GROUPS = 8
PATCHES = 4
PATCH_MAX = 256
SEQ = 768
TICKS = 4
SECTIONS = 32


def draw_segment_starting_activations(key, part):
    key = jax.random.fold_in(key, 11)
    key_base, key_rows, key_cols = jax.random.split(key, 3)
    base_draw = jnp.clip(jax.random.normal(key_base, (SECTIONS, PATCH_MAX, D), jnp.float32), -4.0, 4.0)
    low_end = 0.3
    high_end = 3.0
    row_scale = jnp.exp(jax.random.uniform(key_rows, (SECTIONS, PATCH_MAX, 1), jnp.float32, math.log(low_end), math.log(high_end)))
    col_scale = jnp.exp(jax.random.uniform(key_cols, (1, 1, D), jnp.float32, math.log(low_end), math.log(high_end)))
    return (base_draw * row_scale * col_scale).astype(jnp.bfloat16)


def level_of(own_key, shape, cuts, least, top_value):
    level = 1.0
    for position, blocks in cuts:
        steps = jax.random.uniform(jax.random.fold_in(jax.random.fold_in(own_key, 6), position), (blocks,), jnp.float32, least / len(cuts), top_value / len(cuts))
        level = level * jnp.repeat(jnp.exp(steps), shape[position] // blocks).reshape((-1,) + (1,) * (len(shape) - 1 - position))
    return level


def split_up(count, total, most, skew):
    weights = [(1 << 20) // math.isqrt(standing ** skew) + 1 for standing in range(2, count + 1)]
    rest, given = total - most - (count - 1), [1] * (count - 1)
    while rest > 0:
        candidates = [i for i in range(count - 1) if given[i] < most]
        whole, remaining = sum([weights[i] for i in candidates]), rest
        for i in candidates:
            addition = min(most - given[i], max(1, remaining * weights[i] // whole), rest)
            given[i] = given[i] + addition
            rest = rest - addition
    return np.array([most] + given)


def ragged(own_key, amount, total, bound, slope):
    if amount == 2:
        one = jax.random.randint(own_key, (), max(1, total - bound), min(bound, total - 1) + 1)
        return jnp.stack([one, total - one])
    sizes = jnp.asarray(split_up(amount, total, bound, slope), jnp.int32)
    pairs = (amount - 1) // 2
    donor, receiver = sizes[1:1 + 2 * pairs:2], sizes[2:2 + 2 * pairs:2]
    room = jnp.minimum(donor - 1, bound - receiver)
    shifted = jax.random.randint(jax.random.fold_in(own_key, 1), (pairs,), 0, 1 << 20) % (room + 1)
    sizes = sizes.at[1:1 + 2 * pairs:2].set(donor - shifted).at[2:2 + 2 * pairs:2].set(receiver + shifted)
    return sizes[jax.random.permutation(jax.random.fold_in(own_key, 2), amount)]


def scatter_about(own_key, shape, scale, most, cuts=(), held_as=jnp.bfloat16):
    entries = jax.random.normal(own_key, shape, jnp.float32) * scale
    if len(cuts) > 0:
        entries = level_of(own_key, shape, cuts, -0.22, 0.18) * entries
    return jnp.clip(entries, min=-most, max=most).astype(held_as)


def setup_inputs(seed: int = 0) -> dict:
    streams_of = jax.random.split(jax.random.key(seed), 8)
    segment_starting_activations = draw_segment_starting_activations(jax.random.fold_in(streams_of[7], 71), 0)
    prior_step_memory_pairs = scatter_about(streams_of[1], (SECTIONS, 2, SEQ, INNER), 1.0, 3.0, ((0, 32), (3, 8)))
    triple_projection_matrix = scatter_about(streams_of[2], (SECTIONS, D, 3, INNER), D ** -0.5, 0.125, ((0, 32), (3, 8)))
    final_projection_matrix = scatter_about(streams_of[3], (SECTIONS, INNER, D), INNER ** -0.5, 0.109375, ((0, 32), (1, 8)))
    layer_gain_factors = jnp.clip(jnp.exp(math.log(2.0) - 1.3862944 * jax.random.uniform(streams_of[4], (SECTIONS, D), jnp.float32) ** level_of(streams_of[4], (SECTIONS, D), ((0, 32),), -0.2, 0.2)), 0.5, 2.0)
    tile_element_counts = ragged(streams_of[5], PATCHES, SEQ, PATCH_MAX, 1).astype(jnp.int32)
    tile_visit_order = jax.random.permutation(streams_of[6], PATCHES).astype(jnp.int32)
    return dict(segment_starting_activations=segment_starting_activations, prior_step_memory_pairs=prior_step_memory_pairs, triple_projection_matrix=triple_projection_matrix, final_projection_matrix=final_projection_matrix, layer_gain_factors=layer_gain_factors, tile_element_counts=tile_element_counts, tile_visit_order=tile_visit_order)


SCORE_GAIN = 2.5
EPSILON = 1e-06

def rms_rows(values, gain_row):
    widened = values.astype(jnp.float32)
    spread = lax.optimization_barrier(jnp.mean(widened * widened, axis=-1, keepdims=True))
    return (widened * lax.rsqrt(spread + EPSILON) * gain_row).astype(jnp.bfloat16)

def plan(lengths, order, section_id, tick_step):
    slot_ids = jnp.arange(lengths.shape[0], dtype=jnp.int32)
    slot_id = (section_id - tick_step) % lengths.shape[0]
    patch_id = jnp.sum(jnp.where(slot_ids == slot_id, order, 0))
    length = jnp.sum(jnp.where(slot_ids == patch_id, lengths, 0))
    first_row = jnp.sum(jnp.where(slot_ids < patch_id, lengths, 0))
    return (first_row.astype(jnp.int32), length)

def head_norm(values, head_count):
    shaped = values.reshape(values.shape[0], head_count, HD)
    spread = lax.optimization_barrier(jnp.mean(shaped * shaped, axis=-1, keepdims=True))
    return (shaped * lax.rsqrt(spread + EPSILON)).astype(jnp.bfloat16)

def refresh(kv_store, fresh, first_row, length):
    summed = kv_store.shape[1]
    padded = jnp.concatenate([kv_store, jnp.zeros_like(fresh)], axis=1)
    window = lax.dynamic_slice_in_dim(padded, first_row, fresh.shape[1], 1)
    keep_rows = jnp.arange(fresh.shape[1], dtype=jnp.int32) < length
    window = jnp.where(keep_rows[None, :, None], fresh, window)
    padded = lax.dynamic_update_slice_in_dim(padded, window, first_row, 1)
    return padded[:, :summed]

def section_pass(x_rows, kv_store, w_qkv, w_out, gain_row, section_id, tick_step, tile_element_counts, tile_visit_order):
    first_row, length = plan(tile_element_counts, tile_visit_order, section_id, tick_step)
    normed = rms_rows(x_rows, gain_row)
    projected = jnp.dot(normed, w_qkv.reshape(D, 3 * INNER), preferred_element_type=jnp.float32)
    queries = head_norm(projected[:, :INNER], HEADS)
    key_new = head_norm(projected[:, INNER:2 * INNER], HEADS).reshape(-1, INNER)
    value_new = projected[:, 2 * INNER:].astype(jnp.bfloat16)
    kv_store = refresh(kv_store, jnp.stack([key_new, value_new]), first_row, length)
    key_all = kv_store[0].reshape(-1, HEADS, HD).astype(jnp.float32)
    value_all = kv_store[1].reshape(-1, HEADS, HD).astype(jnp.float32)
    scores = jnp.einsum('qhd,khd->hqk', queries.astype(jnp.float32), key_all) * (SCORE_GAIN / math.sqrt(HD))
    weights = jnp.exp(scores)
    probabilities = (weights / lax.optimization_barrier(jnp.sum(weights, axis=-1, keepdims=True))).astype(jnp.bfloat16)
    attended = jnp.einsum('hqk,khd->qhd', probabilities.astype(jnp.float32), value_all)
    attended = attended.astype(jnp.bfloat16).reshape(-1, INNER)
    grouped = attended.reshape(-1, GROUPS, INNER // GROUPS).astype(jnp.float32)
    w_grouped = w_out.reshape(GROUPS, INNER // GROUPS, D).astype(jnp.float32)
    partial_value = jnp.einsum('qgc,gcd->gqd', grouped, w_grouped)
    partial_value = lax.optimization_barrier(partial_value.astype(jnp.bfloat16)).astype(jnp.float32)
    summed = lax.optimization_barrier(jnp.sum(partial_value, axis=0))
    return ((x_rows.astype(jnp.float32) + summed).astype(jnp.bfloat16), kv_store)

def reference(segment_starting_activations, prior_step_memory_pairs, triple_projection_matrix, final_projection_matrix, layer_gain_factors, tile_element_counts, tile_visit_order):
    segment_indices = jnp.arange(SECTIONS, dtype=jnp.int32)
    for tick_step in range(TICKS):

        def run_relay_segment(packed):
            section_id, x_rows, kv_store, w_qkv, w_out, gain_row = packed
            return section_pass(x_rows, kv_store, w_qkv, w_out, gain_row, section_id, tick_step, tile_element_counts, tile_visit_order)
        rotated_entries, prior_step_memory_pairs = lax.map(run_relay_segment, (segment_indices, segment_starting_activations, prior_step_memory_pairs, triple_projection_matrix, final_projection_matrix, layer_gain_factors))
        segment_starting_activations = jnp.roll(rotated_entries, 1, axis=0)
    return (segment_starting_activations, prior_step_memory_pairs)
```

```python
import functools
import math

import jax
import jax.numpy as jnp
from jax import lax
from jax.experimental import pallas as pl
from jax.experimental.pallas import tpu as pltpu
from jax.sharding import PartitionSpec as P

HD = 128
TICKS = 4
SCORE_GAIN = 2.5
EPSILON = 1e-06
PIECE = 16
SHIFT = 16.0
MESH = pl.DeviceIdType.MESH


def relay_kernel(
    n_sections, counts_ref, order_ref, x0_ref, kv_hbm, wqkv_hbm, wout_hbm, gain_ref, out_ref, kv_out,
    X, PA, R3, RL, EX, S, W, WO, KV, Q, KF, VF, O, L, wsem, xsem, ss, zs, zs0, r3s, rls, exs, ags, osem,
):
    model = X.shape[-1]
    inner = KV.shape[-1]
    heads = inner // HD
    tokens = KV.shape[1]
    NP = PA.shape[1]
    NB = NP // 2
    rows = 4 * PIECE
    patches = order_ref.shape[0]

    section, sp = lax.axis_index("section"), lax.axis_index("sp")
    zh, y = sp // 4, sp % 4
    later, before = (section + 1) % n_sections, (section + n_sections - 1) % n_sections
    up, down = (section, zh * 4 + (y + 1) % 4), (section, zh * 4 + (y + 3) % 4)
    across = (section, (1 - zh) * 4 + y)
    next_same, next_other = (later, zh * 4 + y), (later, (1 - zh) * 4 + y)

    def send(src, dst, send_sem, recv_sem, device):
        pltpu.make_async_remote_copy(
            src_ref=src, dst_ref=dst, send_sem=send_sem, recv_sem=recv_sem, device_id=device, device_id_type=MESH
        ).start()

    def take(view, sem):
        pltpu.make_async_copy(view, view, sem).wait()

    def take_pieces(count, sem):
        take(X.at[pl.ds(0, count // 4)] if count % 4 == 0 else X.at[0, pl.ds(0, count)], sem)

    loads = [pltpu.make_async_copy(kv_hbm.at[0], KV, wsem.at[4])]
    for j in range(3):
        loads.append(pltpu.make_async_copy(wqkv_hbm.at[0, j], W.at[:, pl.ds(j * inner, inner)], wsem.at[j]))
    loads.append(pltpu.make_async_copy(wout_hbm.at[0], WO, wsem.at[3]))
    starts = [
        pltpu.make_async_copy(x0_ref.at[0, pl.ds(k * PIECE, PIECE)], X.at[zh * NB + k, 0], xsem.at[k]) for k in range(NB)
    ]
    for copy in starts + loads:
        copy.start()

    barrier = pltpu.get_barrier_semaphore()
    friends = [up, down, across, next_same, next_other, (before, zh * 4 + y), (before, (1 - zh) * 4 + y)]
    for device in friends:
        pl.semaphore_signal(barrier, inc=1, device_id=device, device_id_type=MESH)
    pl.semaphore_wait(barrier, len(friends))

    for copy in starts:
        copy.wait()
    for k in range(NB):
        piece = X.at[zh * NB + k, 0]
        send(piece, piece, zs0, exs.at[0, zh * NB + k], across)
    for copy in loads:
        copy.wait()

    local = lax.broadcasted_iota(jnp.int32, (1, NP * rows), 1)
    slot = (local % rows) // PIECE
    chunk = (y + jnp.where(slot == 1, 1, jnp.where(slot == 2, 3, jnp.where(slot == 3, 2, 0)))) % 4
    within = (local // rows) * PIECE + local % PIECE
    global_row = (within // 32) * 128 + chunk * 32 + within % 32
    token = lax.broadcasted_iota(jnp.int32, (1, tokens), 1)
    gain = gain_ref[...]
    factor = SCORE_GAIN / math.sqrt(HD) * math.log2(math.e)
    shift = SHIFT * math.log2(math.e)

    def head_norm(part):
        spread = jnp.mean(part * part, axis=-1, keepdims=True)
        return (part * lax.rsqrt(spread + EPSILON)).astype(jnp.bfloat16)

    def scores(query, keys, bias):
        s = lax.dot_general(query, keys, (((1,), (1,)), ((), ())), preferred_element_type=jnp.float32)
        return jnp.exp2(s * factor + bias)

    def tick(t, _):
        patch = order_ref[(section + TICKS * n_sections - t) % patches]
        length, first = jnp.int32(0), jnp.int32(0)
        for r in range(patches):
            length = length + jnp.where(patch == r, counts_ref[r], 0)
            first = first + jnp.where(r < patch, counts_ref[r], 0)
        held_bias = jnp.where((token >= first) & (token < first + length), -1e30, -shift)
        fresh_bias = jnp.where(global_row < length, -shift, -1e30)

        def place(i):
            return (i + jnp.where(t == 0, zh * NB, 0)) % NP

        def stage_f(i):
            ii = place(i)
            if i >= NB:
                @pl.when(t == 0)
                def _():
                    take(X.at[ii, 0], exs.at[0, ii])

            @pl.when(t > 0)
            def _():
                take(EX.at[t, i], exs.at[t, i])
                total = EX[t, i, 0].astype(jnp.float32) + EX[t, i, 1].astype(jnp.float32)
                X[t * NP + ii, 0] = total.astype(jnp.bfloat16)

            at = t * NP + ii
            send(X.at[at, 0], X.at[at, 2], ss.at[t], ags.at[t, ii, 2], up)
            send(X.at[at, 0], X.at[at, 1], ss.at[t], ags.at[t, ii, 1], down)

        def stage_g(i):
            ii = place(i)
            at = t * NP + ii
            source, device = (2, up) if i % 2 == 0 else (1, down)
            take(X.at[at, source], ags.at[t, ii, source])
            send(X.at[at, source], X.at[at, 3], ss.at[t], ags.at[t, ii, 3], device)

        def stage_h(i):
            ii = place(i)
            at = t * NP + ii
            other = 1 if i % 2 == 0 else 2
            take(X.at[at, other], ags.at[t, ii, other])
            take(X.at[at, 3], ags.at[t, ii, 3])
            x = X[at].reshape(rows, model).astype(jnp.float32)
            spread = jnp.mean(x * x, axis=-1, keepdims=True)
            normed = (x * lax.rsqrt(spread + EPSILON) * gain).astype(jnp.bfloat16)
            here = pl.ds(pl.multiple_of(ii * rows, rows), rows)
            parts = [
                jnp.dot(normed, W[:, j * inner : (j + 1) * inner], preferred_element_type=jnp.float32) for j in range(3)
            ]
            VF[here, :] = parts[2].astype(jnp.bfloat16)
            for h in range(heads):
                cols = slice(h * HD, (h + 1) * HD)
                query = head_norm(parts[0][:, cols])
                Q[here, cols] = query
                KF[here, cols] = head_norm(parts[1][:, cols])
                e = scores(query, KV[0, :, cols], held_bias)
                L[here, cols] = jnp.broadcast_to(jnp.sum(e, axis=-1, keepdims=True), (rows, HD))
                O[here, cols] = jnp.dot(e.astype(jnp.bfloat16), KV[1, :, cols], preferred_element_type=jnp.float32)

        def stage_c(i):
            here = slice(i * rows, (i + 1) * rows)
            attended = []
            for h in range(heads):
                cols = slice(h * HD, (h + 1) * HD)
                e = scores(Q[here, cols], KF[:, cols], fresh_bias)
                total = L[here, cols] + jnp.sum(e, axis=-1, keepdims=True)
                mixed = O[here, cols] + jnp.dot(
                    e.astype(jnp.bfloat16), VF[:, cols], preferred_element_type=jnp.float32
                )
                attended.append((mixed / total).astype(jnp.bfloat16))
            partial = jnp.dot(jnp.concatenate(attended, axis=1), WO[...], preferred_element_type=jnp.float32)
            PA[t, i] = partial.astype(jnp.bfloat16).reshape(4, PIECE, model)
            if i % 2 == 0:
                send(PA.at[t, i, 3], R3.at[t, i], ss.at[t], r3s.at[t, i], up)
                send(PA.at[t, i, 2], RL.at[t, i, 1], ss.at[t], rls.at[t, i], down)
            else:
                send(PA.at[t, i, 3], R3.at[t, i], ss.at[t], r3s.at[t, i], down)
                send(PA.at[t, i, 1], RL.at[t, i, 0], ss.at[t], rls.at[t, i], up)

        def stage_d(i):
            take(R3.at[t, i], r3s.at[t, i])
            mine, side, device = (1, 0, up) if i % 2 == 0 else (2, 1, down)
            total = PA[t, i, mine].astype(jnp.float32) + R3[t, i].astype(jnp.float32)
            PA[t, i, mine] = total.astype(jnp.bfloat16)
            send(PA.at[t, i, mine], RL.at[t, i, side], ss.at[t], rls.at[t, i], device)

        def stage_e(i):
            take(RL.at[t, i], rls.at[t, i])
            total = PA[t, i, 0].astype(jnp.float32) + RL[t, i, 0].astype(jnp.float32) + RL[t, i, 1].astype(jnp.float32)
            total = total + jnp.where(zh == i // NB, X[t * NP + i, 0].astype(jnp.float32), 0.0)
            S[t, i] = total.astype(jnp.bfloat16)

            @pl.when(t < TICKS - 1)
            def _():
                send(S.at[t, i], EX.at[t + 1, i, 0], zs.at[t], exs.at[t + 1, i], next_same)
                send(S.at[t, i], EX.at[t + 1, i, 1], zs.at[t], exs.at[t + 1, i], next_other)

            @pl.when(t == TICKS - 1)
            def _():
                k = i % NB
                send(S.at[t, i], EX.at[TICKS, k, zh], zs.at[t], exs.at[TICKS, k], (later, (i // NB) * 4 + y))

        def update():
            for b in range(3):
                span = tokens // 3
                at = pl.ds(b * span, span)
                row = lax.broadcasted_iota(jnp.int32, (span, 1), 0) + (b * span - first)
                hit = (row == global_row) & (global_row < length)
                pick = jnp.where(hit, 1.0, 0.0).astype(jnp.bfloat16)
                inside = (row >= 0) & (row < length)
                for part, fresh in ((0, KF), (1, VF)):
                    moved = jnp.dot(pick, fresh[...], preferred_element_type=jnp.float32)
                    kept = KV[part, at, :].astype(jnp.float32)
                    KV[part, at, :] = jnp.where(inside, moved, kept).astype(jnp.bfloat16)

        stage_f(0)
        for i in range(1, NP):
            stage_f(i)
            stage_g(i - 1)
            if i >= 2:
                stage_h(i - 2)
        stage_g(NP - 1)
        stage_h(NP - 2)
        stage_h(NP - 1)
        for i in range(NP):
            stage_c(i)
        stage_d(0)
        for i in range(1, NP):
            stage_d(i)
            stage_e(i - 1)
        stage_e(NP - 1)
        update()
        return 0

    lax.fori_loop(0, TICKS, tick, 0)
    cache_out = pltpu.make_async_copy(KV, kv_out.at[0], osem)
    cache_out.start()
    for k in range(NB):
        take(EX.at[TICKS, k], exs.at[TICKS, k])
        total = EX[TICKS, k, 0].astype(jnp.float32) + EX[TICKS, k, 1].astype(jnp.float32)
        out_ref[0, pl.ds(k * PIECE, PIECE), :] = total.astype(jnp.bfloat16)
    take_pieces(NB, zs0)
    for t in range(TICKS):
        take_pieces(6 * NP, ss.at[t])
        take_pieces(2 * NP if t < TICKS - 1 else NP, zs.at[t])
    cache_out.wait()


def local(n_sections, x0, kv, wqkv, wout, gain, counts, order):
    entries, model = x0.shape[1:]
    tokens, inner = kv.shape[2:]
    NP = 2 * entries // PIECE
    NB = NP // 2
    rows = 8 * entries
    bf16, f32 = jnp.bfloat16, jnp.float32
    piece = (PIECE, model)
    dma = pltpu.SemaphoreType.DMA
    any_space = pl.BlockSpec(memory_space=pl.ANY)
    vmem = pl.BlockSpec(memory_space=pltpu.VMEM)
    smem = pl.BlockSpec(memory_space=pltpu.SMEM)
    return pl.pallas_call(
        functools.partial(relay_kernel, n_sections),
        out_shape=(
            jax.ShapeDtypeStruct((1, entries, model), bf16),
            jax.ShapeDtypeStruct((1, 2, tokens, inner), bf16),
        ),
        in_specs=[smem, smem, any_space, any_space, any_space, any_space, vmem],
        out_specs=(vmem, any_space),
        scratch_shapes=[
            pltpu.VMEM((TICKS * NP, 4) + piece, bf16),
            pltpu.VMEM((TICKS, NP, 4) + piece, bf16),
            pltpu.VMEM((TICKS, NP) + piece, bf16),
            pltpu.VMEM((TICKS, NP, 2) + piece, bf16),
            pltpu.VMEM((TICKS + 1, NP, 2) + piece, bf16),
            pltpu.VMEM((TICKS, NP) + piece, bf16),
            pltpu.VMEM((model, 3 * inner), bf16),
            pltpu.VMEM((inner, model), bf16),
            pltpu.VMEM((2, tokens, inner), bf16),
            pltpu.VMEM((rows, inner), bf16),
            pltpu.VMEM((rows, inner), bf16),
            pltpu.VMEM((rows, inner), bf16),
            pltpu.VMEM((rows, inner), f32),
            pltpu.VMEM((rows, inner), f32),
            dma((5,)), dma((NB,)), dma((TICKS,)), dma((TICKS,)), dma,
            dma((TICKS, NP)), dma((TICKS, NP)), dma((TICKS + 1, NP)), dma((TICKS, NP, 4)), dma,
        ],
        compiler_params=pltpu.CompilerParams(
            collective_id=0, has_side_effects=True, vmem_limit_bytes=56 * 1024 * 1024
        ),
    )(counts, order, x0, kv, jnp.transpose(wqkv, (0, 2, 1, 3)), wout, gain)


def solution(mesh):
    placed = (
        P("section", "sp", None),
        P("section", None, None, "sp"),
        P("section", None, None, "sp"),
        P("section", "sp", None),
        P("section", None),
        P(),
        P(),
    )
    return jax.shard_map(
        functools.partial(local, mesh.shape["section"]),
        mesh=mesh,
        in_specs=placed,
        out_specs=(P("section", "sp", None), P("section", None, None, "sp")),
        check_vma=False,
    )
```

```python
import functools
import math

import jax
import jax.numpy as jnp
from jax import lax
from jax.experimental import pallas as pl
from jax.experimental.pallas import tpu as pltpu
from jax.sharding import PartitionSpec as P

HD = 128
TICKS = 4
SCORE_GAIN = 2.5
EPSILON = 1e-06
PIECE = 16
SHIFT = 16.0
MESH = pl.DeviceIdType.MESH
CUTS = 2
HEAD = ("h0", "h1", "h2", "k3")
TAIL = ("c0", "q", "c1", "c2", "c3", "e0", "e1", "e2", "f0", "e3", "f1", "u", "f2", "f3")


def relay_kernel(
    n_sections, counts_ref, order_ref, x0_ref, kv_hbm, wqkv_hbm, wout_hbm, gain_ref, out_ref, kv_out,
    X, PA, RL, EX, S, W, WO, KV, Q, KF, VF, O, L, wsem, xsem, ss, zs, zs0, rls, exs, ags, osem,
):
    model = X.shape[-1]
    inner = KV.shape[-1]
    heads = inner // HD
    tokens = KV.shape[1]
    NP = PA.shape[1]
    NB = NP // 2
    rows = 4 * PIECE
    width = model // CUTS
    patches = order_ref.shape[0]

    section, sp = lax.axis_index("section"), lax.axis_index("sp")
    zh, y = sp // 4, sp % 4
    later, before = (section + 1) % n_sections, (section + n_sections - 1) % n_sections
    up, down = (section, zh * 4 + (y + 1) % 4), (section, zh * 4 + (y + 3) % 4)
    across = (section, (1 - zh) * 4 + y)
    opposite = (section, zh * 4 + (y + 2) % 4)
    next_same, next_other = (later, zh * 4 + y), (later, (1 - zh) * 4 + y)

    def send(src, dst, send_sem, recv_sem, device):
        pltpu.make_async_remote_copy(
            src_ref=src, dst_ref=dst, send_sem=send_sem, recv_sem=recv_sem, device_id=device, device_id_type=MESH
        ).start()

    def take(view, sem):
        pltpu.make_async_copy(view, view, sem).wait()

    def take_pieces(count, sem):
        take(X.at[pl.ds(0, count // 4)] if count % 4 == 0 else X.at[0, pl.ds(0, count)], sem)

    loads = [pltpu.make_async_copy(kv_hbm.at[0], KV, wsem.at[4])]
    for j in range(3):
        loads.append(pltpu.make_async_copy(wqkv_hbm.at[0, j], W.at[:, pl.ds(j * inner, inner)], wsem.at[j]))
    loads.append(pltpu.make_async_copy(wout_hbm.at[0], WO, wsem.at[3]))
    starts = [
        pltpu.make_async_copy(x0_ref.at[0, pl.ds(k * PIECE, PIECE)], X.at[zh * NB + k, 0], xsem.at[k]) for k in range(NB)
    ]
    for copy in starts + loads:
        copy.start()

    barrier = pltpu.get_barrier_semaphore()
    friends = [up, down, opposite, across, next_same, next_other, (before, zh * 4 + y), (before, (1 - zh) * 4 + y)]
    for device in friends:
        pl.semaphore_signal(barrier, inc=1, device_id=device, device_id_type=MESH)
    pl.semaphore_wait(barrier, len(friends))

    for copy in starts:
        copy.wait()
    for k in range(NB):
        piece = X.at[zh * NB + k, 0]
        send(piece, piece, zs0, exs.at[0, zh * NB + k, 0], across)
    local = lax.broadcasted_iota(jnp.int32, (1, NP * rows), 1)
    slot = (local % rows) // PIECE
    chunk = (y + jnp.where(slot == 1, 1, jnp.where(slot == 2, 3, jnp.where(slot == 3, 2, 0)))) % 4
    within = (local // rows) * PIECE + local % PIECE
    global_row = (within // 32) * 128 + chunk * 32 + within % 32
    token = lax.broadcasted_iota(jnp.int32, (1, tokens), 1)
    gain = gain_ref[...]
    factor = SCORE_GAIN / math.sqrt(HD) * math.log2(math.e)
    shift = SHIFT * math.log2(math.e)

    def gather(t, at, i, c):
        spot = pl.ds(c * width, width)
        for k, device in ((2, up), (1, down), (3, opposite)):
            send(X.at[at, 0, :, spot], X.at[at, k, :, spot], ss.at[t], ags.at[t, i, k], device)

    for i in range(NP):
        ii = (i + zh * NB) % NP
        if i >= NB:
            take(X.at[ii, 0], exs.at[0, ii, 0])
        for c in range(CUTS):
            gather(0, ii, ii, c)
    for copy in loads:
        copy.wait()

    def head_norm(part):
        spread = jnp.mean(part * part, axis=-1, keepdims=True)
        return (part * lax.rsqrt(spread + EPSILON)).astype(jnp.bfloat16)

    def scores(query, keys, bias):
        s = lax.dot_general(query, keys, (((1,), (1,)), ((), ())), preferred_element_type=jnp.float32)
        return jnp.exp2(s * factor + bias)

    def tick(t, _):
        patch = order_ref[(section + TICKS * n_sections - t) % patches]
        length, first = jnp.int32(0), jnp.int32(0)
        for r in range(patches):
            length = length + jnp.where(patch == r, counts_ref[r], 0)
            first = first + jnp.where(r < patch, counts_ref[r], 0)
        held_bias = jnp.where((token >= first) & (token < first + length), -1e30, -shift)
        fresh_bias = jnp.where(global_row < length, -shift, -1e30)

        def stage_f(i):
            @pl.when(t < TICKS - 1)
            def _():
                at = (t + 1) * NP + i
                for c in range(CUTS):
                    part = slice(c * width, (c + 1) * width)
                    take(EX.at[t + 1, i, :, :, pl.ds(c * width, width)], exs.at[t + 1, i, c])
                    total = EX[t + 1, i, 0, :, part].astype(jnp.float32) + EX[t + 1, i, 1, :, part].astype(jnp.float32)
                    X[at, 0, :, part] = total.astype(jnp.bfloat16)
                    gather(t + 1, at, i, c)

        def stage_h(i, whole=True):
            at = t * NP + i
            for k in (1, 2, 3):
                take(X.at[at, k], ags.at[t, i, k])
            x = X[at].reshape(rows, model).astype(jnp.float32)
            spread = jnp.mean(x * x, axis=-1, keepdims=True)
            normed = (x * lax.rsqrt(spread + EPSILON) * gain).astype(jnp.bfloat16)
            here = slice(i * rows, (i + 1) * rows)

            def project(j):
                return jnp.dot(normed, W[:, j * inner : (j + 1) * inner], preferred_element_type=jnp.float32)

            VF[here, :] = project(2).astype(jnp.bfloat16)
            keys = project(1)
            for h in range(heads):
                cols = slice(h * HD, (h + 1) * HD)
                KF[here, cols] = head_norm(keys[:, cols])

            def finish():
                queries = project(0)
                for h in range(heads):
                    cols = slice(h * HD, (h + 1) * HD)
                    query = head_norm(queries[:, cols])
                    Q[here, cols] = query
                    e = scores(query, KV[0, :, cols], held_bias)
                    L[here, cols] = jnp.broadcast_to(jnp.sum(e, axis=-1, keepdims=True), (rows, HD))
                    O[here, cols] = jnp.dot(e.astype(jnp.bfloat16), KV[1, :, cols], preferred_element_type=jnp.float32)

            if whole:
                finish()
            return finish

        def stage_c(i):
            here = slice(i * rows, (i + 1) * rows)
            attended = []
            for h in range(heads):
                cols = slice(h * HD, (h + 1) * HD)
                e = scores(Q[here, cols], KF[:, cols], fresh_bias)
                total = L[here, cols] + jnp.sum(e, axis=-1, keepdims=True)
                mixed = O[here, cols] + jnp.dot(
                    e.astype(jnp.bfloat16), VF[:, cols], preferred_element_type=jnp.float32
                )
                attended.append((mixed / total).astype(jnp.bfloat16))
            attended = jnp.concatenate(attended, axis=1)
            for c in range(CUTS):
                part = slice(c * width, (c + 1) * width)
                spot = pl.ds(c * width, width)
                partial = jnp.dot(attended, WO[:, part], preferred_element_type=jnp.float32)
                PA[t, i, :, :, part] = partial.astype(jnp.bfloat16).reshape(4, PIECE, width)
                for k, device in ((3, opposite), (1, up), (2, down)):
                    send(PA.at[t, i, k, :, spot], RL.at[t, i, k - 1, :, spot], ss.at[t], rls.at[t, i, c], device)

        def stage_e(i):
            for c in range(CUTS):
                part = slice(c * width, (c + 1) * width)
                spot = pl.ds(c * width, width)
                take(RL.at[t, i, :, :, spot], rls.at[t, i, c])
                total = PA[t, i, 0, :, part].astype(jnp.float32)
                for k in range(3):
                    total = total + RL[t, i, k, :, part].astype(jnp.float32)
                total = total + jnp.where(zh == i // NB, X[t * NP + i, 0, :, part].astype(jnp.float32), 0.0)
                S[t, i, :, part] = total.astype(jnp.bfloat16)
                mine = S.at[t, i, :, spot]

                @pl.when(t < TICKS - 1)
                def _():
                    send(mine, EX.at[t + 1, i, 1, :, spot], zs.at[t], exs.at[t + 1, i, c], next_other)
                    send(mine, EX.at[t + 1, i, 0, :, spot], zs.at[t], exs.at[t + 1, i, c], next_same)

                @pl.when(t == TICKS - 1)
                def _():
                    k = i % NB
                    target = (later, (i // NB) * 4 + y)
                    send(mine, EX.at[TICKS, k, zh, :, spot], zs.at[t], exs.at[TICKS, k, c], target)

        def update():
            for b in range(3):
                span = tokens // 3
                at = pl.ds(b * span, span)
                row = lax.broadcasted_iota(jnp.int32, (span, 1), 0) + (b * span - first)
                hit = (row == global_row) & (global_row < length)
                pick = jnp.where(hit, 1.0, 0.0).astype(jnp.bfloat16)
                inside = (row >= 0) & (row < length)
                for part, fresh in ((0, KF), (1, VF)):
                    moved = jnp.dot(pick, fresh[...], preferred_element_type=jnp.float32)
                    kept = KV[part, at, :].astype(jnp.float32)
                    KV[part, at, :] = jnp.where(inside, moved, kept).astype(jnp.bfloat16)

        stages = dict(h=stage_h, c=stage_c, e=stage_e, f=stage_f)
        finish = None
        for step in HEAD + TAIL:
            kind, i = step[0], int(step[1:] or 0)
            if kind == "k":
                finish = stage_h(i, False)
            elif kind == "q":
                finish()
            elif kind == "u":
                update()
            else:
                stages[kind](i)
        return 0

    lax.fori_loop(0, TICKS, tick, 0)
    cache_out = pltpu.make_async_copy(KV, kv_out.at[0], osem)
    cache_out.start()
    for k in range(NB):
        for c in range(CUTS):
            part = slice(c * width, (c + 1) * width)
            take(EX.at[TICKS, k, :, :, pl.ds(c * width, width)], exs.at[TICKS, k, c])
            total = EX[TICKS, k, 0, :, part].astype(jnp.float32) + EX[TICKS, k, 1, :, part].astype(jnp.float32)
            out_ref[0, pl.ds(k * PIECE, PIECE), part] = total.astype(jnp.bfloat16)
    take_pieces(NB, zs0)
    for t in range(TICKS):
        take_pieces(6 * NP, ss.at[t])
        take_pieces(2 * NP if t < TICKS - 1 else NP, zs.at[t])
    cache_out.wait()


def local(n_sections, x0, kv, wqkv, wout, gain, counts, order):
    entries, model = x0.shape[1:]
    tokens, inner = kv.shape[2:]
    NP = 2 * entries // PIECE
    NB = NP // 2
    rows = 8 * entries
    bf16, f32 = jnp.bfloat16, jnp.float32
    piece = (PIECE, model)
    dma = pltpu.SemaphoreType.DMA
    any_space = pl.BlockSpec(memory_space=pl.ANY)
    vmem = pl.BlockSpec(memory_space=pltpu.VMEM)
    smem = pl.BlockSpec(memory_space=pltpu.SMEM)
    return pl.pallas_call(
        functools.partial(relay_kernel, n_sections),
        out_shape=(
            jax.ShapeDtypeStruct((1, entries, model), bf16),
            jax.ShapeDtypeStruct((1, 2, tokens, inner), bf16),
        ),
        in_specs=[smem, smem, any_space, any_space, any_space, any_space, vmem],
        out_specs=(vmem, any_space),
        scratch_shapes=[
            pltpu.VMEM((TICKS * NP, 4) + piece, bf16),
            pltpu.VMEM((TICKS, NP, 4) + piece, bf16),
            pltpu.VMEM((TICKS, NP, 3) + piece, bf16),
            pltpu.VMEM((TICKS + 1, NP, 2) + piece, bf16),
            pltpu.VMEM((TICKS, NP) + piece, bf16),
            pltpu.VMEM((model, 3 * inner), bf16),
            pltpu.VMEM((inner, model), bf16),
            pltpu.VMEM((2, tokens, inner), bf16),
            pltpu.VMEM((rows, inner), bf16),
            pltpu.VMEM((rows, inner), bf16),
            pltpu.VMEM((rows, inner), bf16),
            pltpu.VMEM((rows, inner), f32),
            pltpu.VMEM((rows, inner), f32),
            dma((5,)), dma((NB,)), dma((TICKS,)), dma((TICKS,)), dma,
            dma((TICKS, NP, CUTS)), dma((TICKS + 1, NP, CUTS)), dma((TICKS, NP, 4)), dma,
        ],
        compiler_params=pltpu.CompilerParams(
            collective_id=0, has_side_effects=True, vmem_limit_bytes=56 * 1024 * 1024
        ),
    )(counts, order, x0, kv, jnp.transpose(wqkv, (0, 2, 1, 3)), wout, gain)


def solution(mesh):
    placed = (
        P("section", "sp", None),
        P("section", None, None, "sp"),
        P("section", None, None, "sp"),
        P("section", "sp", None),
        P("section", None),
        P(),
        P(),
    )
    return jax.shard_map(
        functools.partial(local, mesh.shape["section"]),
        mesh=mesh,
        in_specs=placed,
        out_specs=(P("section", "sp", None), P("section", None, None, "sp")),
        check_vma=False,
    )
```

```python
import functools
import math

import jax
import jax.numpy as jnp
from jax import lax
from jax.experimental import pallas as pl
from jax.experimental.pallas import tpu as pltpu
from jax.sharding import PartitionSpec as P

HD = 128
TICKS = 4
SCORE_GAIN = 2.5
EPSILON = 1e-06
PIECE = 16
SHIFT = 16.0
MESH = pl.DeviceIdType.MESH
CUTS = 2
HEAD = ("h0", "h1", "h2", "k3")
TAIL = ("c0", "q", "c1", "c2", "c3", "e0", "e1", "e2", "f0", "e3", "f1", "u", "f2", "f3")


def relay_kernel(
    n_sections, counts_ref, order_ref, x0_ref, kv_hbm, wqkv_hbm, wout_hbm, gain_ref, out_ref, kv_out,
    X, PA, RL, EX, S, W, WO, KV, Q, KF, VF, O, L, wsem, xsem, ss, zs, zs0, rls, exs, ags, osem,
):
    model = X.shape[-1]
    inner = KV.shape[-1]
    heads = inner // HD
    tokens = KV.shape[1]
    NP = PA.shape[1]
    NB = NP // 2
    rows = 4 * PIECE
    width = model // CUTS
    patches = order_ref.shape[0]

    section, sp = lax.axis_index("section"), lax.axis_index("sp")
    zh, y = sp // 4, sp % 4
    later, before = (section + 1) % n_sections, (section + n_sections - 1) % n_sections
    up, down = (section, zh * 4 + (y + 1) % 4), (section, zh * 4 + (y + 3) % 4)
    across = (section, (1 - zh) * 4 + y)
    opposite = (section, zh * 4 + (y + 2) % 4)
    next_same, next_other = (later, zh * 4 + y), (later, (1 - zh) * 4 + y)

    def send(src, dst, send_sem, recv_sem, device):
        pltpu.make_async_remote_copy(
            src_ref=src, dst_ref=dst, send_sem=send_sem, recv_sem=recv_sem, device_id=device, device_id_type=MESH
        ).start()

    def take(view, sem):
        pltpu.make_async_copy(view, view, sem).wait()

    def take_pieces(count, sem):
        take(X.at[pl.ds(0, count // 4)] if count % 4 == 0 else X.at[0, pl.ds(0, count)], sem)

    loads = [pltpu.make_async_copy(kv_hbm.at[0], KV, wsem.at[4])]
    for j in range(3):
        loads.append(pltpu.make_async_copy(wqkv_hbm.at[0, j], W.at[:, pl.ds(j * inner, inner)], wsem.at[j]))
    loads.append(pltpu.make_async_copy(wout_hbm.at[0], WO, wsem.at[3]))
    starts = [
        pltpu.make_async_copy(x0_ref.at[0, pl.ds(k * PIECE, PIECE)], X.at[zh * NB + k, 0], xsem.at[k]) for k in range(NB)
    ]
    for copy in starts + loads:
        copy.start()

    barrier = pltpu.get_barrier_semaphore()
    friends = [up, down, opposite, across, next_same, next_other, (before, zh * 4 + y), (before, (1 - zh) * 4 + y)]
    for device in friends:
        pl.semaphore_signal(barrier, inc=1, device_id=device, device_id_type=MESH)
    pl.semaphore_wait(barrier, len(friends))

    for copy in starts:
        copy.wait()
    for k in range(NB):
        for c in range(CUTS):
            piece = X.at[zh * NB + k, 0, :, pl.ds(c * width, width)]
            send(piece, piece, zs0, exs.at[0, zh * NB + k, c], across)
    local = lax.broadcasted_iota(jnp.int32, (1, NP * rows), 1)
    slot = (local % rows) // PIECE
    chunk = (y + jnp.where(slot == 1, 1, jnp.where(slot == 2, 3, jnp.where(slot == 3, 2, 0)))) % 4
    within = (local // rows) * PIECE + local % PIECE
    global_row = (within // 32) * 128 + chunk * 32 + within % 32
    token = lax.broadcasted_iota(jnp.int32, (1, tokens), 1)
    gain = gain_ref[...]
    factor = SCORE_GAIN / math.sqrt(HD) * math.log2(math.e)
    shift = SHIFT * math.log2(math.e)

    def gather(t, at, i, c):
        spot = pl.ds(c * width, width)
        for k, device in ((3, opposite), (2, up), (1, down)):
            send(X.at[at, 0, :, spot], X.at[at, k, :, spot], ss.at[t], ags.at[t, i, k], device)

    for i in range(NP):
        ii = (i + zh * NB) % NP
        for c in range(CUTS):
            if i >= NB:
                take(X.at[ii, 0, :, pl.ds(c * width, width)], exs.at[0, ii, c])
            gather(0, ii, ii, c)
    for copy in loads:
        copy.wait()

    def head_norm(part):
        spread = jnp.mean(part * part, axis=-1, keepdims=True)
        return (part * lax.rsqrt(spread + EPSILON)).astype(jnp.bfloat16)

    def scores(query, keys, bias):
        s = lax.dot_general(query, keys, (((1,), (1,)), ((), ())), preferred_element_type=jnp.float32)
        return jnp.exp2(s * factor + bias)

    def tick(t, _):
        patch = order_ref[(section + TICKS * n_sections - t) % patches]
        length, first = jnp.int32(0), jnp.int32(0)
        for r in range(patches):
            length = length + jnp.where(patch == r, counts_ref[r], 0)
            first = first + jnp.where(r < patch, counts_ref[r], 0)
        held_bias = jnp.where((token >= first) & (token < first + length), -1e30, -shift)
        fresh_bias = jnp.where(global_row < length, -shift, -1e30)

        def stage_f(i):
            @pl.when(t < TICKS - 1)
            def _():
                at = (t + 1) * NP + i
                for c in range(CUTS):
                    part = slice(c * width, (c + 1) * width)
                    take(EX.at[t + 1, i, :, :, pl.ds(c * width, width)], exs.at[t + 1, i, c])
                    total = EX[t + 1, i, 0, :, part].astype(jnp.float32) + EX[t + 1, i, 1, :, part].astype(jnp.float32)
                    X[at, 0, :, part] = total.astype(jnp.bfloat16)
                    gather(t + 1, at, i, c)

        def stage_h(i, whole=True):
            ii = (i + jnp.where(t == 0, zh * NB, 0)) % NP
            at = t * NP + ii
            for k in (1, 2, 3):
                take(X.at[at, k], ags.at[t, ii, k])
            x = X[at].reshape(rows, model).astype(jnp.float32)
            spread = jnp.mean(x * x, axis=-1, keepdims=True)
            normed = (x * lax.rsqrt(spread + EPSILON) * gain).astype(jnp.bfloat16)
            here = pl.ds(pl.multiple_of(ii * rows, rows), rows)

            pairs = jnp.dot(normed, W[:, inner:], preferred_element_type=jnp.float32)
            keys = pairs[:, :inner]
            VF[here, :] = pairs[:, inner:].astype(jnp.bfloat16)
            for h in range(heads):
                cols = slice(h * HD, (h + 1) * HD)
                KF[here, cols] = head_norm(keys[:, cols])

            def finish():
                queries = jnp.dot(normed, W[:, :inner], preferred_element_type=jnp.float32)
                for h in range(heads):
                    cols = slice(h * HD, (h + 1) * HD)
                    query = head_norm(queries[:, cols])
                    Q[here, cols] = query
                    e = scores(query, KV[0, :, cols], held_bias)
                    L[here, cols] = jnp.broadcast_to(jnp.sum(e, axis=-1, keepdims=True), (rows, HD))
                    O[here, cols] = jnp.dot(e.astype(jnp.bfloat16), KV[1, :, cols], preferred_element_type=jnp.float32)

            if whole:
                finish()
            return finish

        def stage_c(i):
            here = slice(i * rows, (i + 1) * rows)
            attended = []
            for h in range(heads):
                cols = slice(h * HD, (h + 1) * HD)
                e = scores(Q[here, cols], KF[:, cols], fresh_bias)
                total = L[here, cols] + jnp.sum(e, axis=-1, keepdims=True)
                mixed = O[here, cols] + jnp.dot(
                    e.astype(jnp.bfloat16), VF[:, cols], preferred_element_type=jnp.float32
                )
                attended.append((mixed / total).astype(jnp.bfloat16))
            attended = jnp.concatenate(attended, axis=1)
            for c in range(CUTS):
                part = slice(c * width, (c + 1) * width)
                spot = pl.ds(c * width, width)
                partial = jnp.dot(attended, WO[:, part], preferred_element_type=jnp.float32)
                PA[t, i, :, :, part] = partial.astype(jnp.bfloat16).reshape(4, PIECE, width)
                for k, device in ((3, opposite), (1, up), (2, down)):
                    send(PA.at[t, i, k, :, spot], RL.at[t, i, k - 1, :, spot], ss.at[t], rls.at[t, i, c], device)

        def stage_e(i):
            for c in range(CUTS):
                part = slice(c * width, (c + 1) * width)
                spot = pl.ds(c * width, width)
                take(RL.at[t, i, :, :, spot], rls.at[t, i, c])
                total = PA[t, i, 0, :, part].astype(jnp.float32)
                for k in range(3):
                    total = total + RL[t, i, k, :, part].astype(jnp.float32)
                total = total + jnp.where(zh == i // NB, X[t * NP + i, 0, :, part].astype(jnp.float32), 0.0)
                S[t, i, :, part] = total.astype(jnp.bfloat16)
                mine = S.at[t, i, :, spot]

                @pl.when(t < TICKS - 1)
                def _():
                    send(mine, EX.at[t + 1, i, 1, :, spot], zs.at[t], exs.at[t + 1, i, c], next_other)
                    send(mine, EX.at[t + 1, i, 0, :, spot], zs.at[t], exs.at[t + 1, i, c], next_same)

                @pl.when(t == TICKS - 1)
                def _():
                    k = i % NB
                    target = (later, (i // NB) * 4 + y)
                    send(mine, EX.at[TICKS, k, zh, :, spot], zs.at[t], exs.at[TICKS, k, c], target)

        def update():
            for b in range(3):
                span = tokens // 3
                at = pl.ds(b * span, span)
                row = lax.broadcasted_iota(jnp.int32, (span, 1), 0) + (b * span - first)
                hit = (row == global_row) & (global_row < length)
                pick = jnp.where(hit, 1.0, 0.0).astype(jnp.bfloat16)
                inside = (row >= 0) & (row < length)
                for part, fresh in ((0, KF), (1, VF)):
                    moved = jnp.dot(pick, fresh[...], preferred_element_type=jnp.float32)
                    kept = KV[part, at, :].astype(jnp.float32)
                    KV[part, at, :] = jnp.where(inside, moved, kept).astype(jnp.bfloat16)

        stages = dict(h=stage_h, c=stage_c, e=stage_e, f=stage_f)
        finish = None
        for step in HEAD + TAIL:
            kind, i = step[0], int(step[1:] or 0)
            if kind == "k":
                finish = stage_h(i, False)
            elif kind == "q":
                finish()
            elif kind == "u":
                update()
            else:
                stages[kind](i)
        return 0

    lax.fori_loop(0, TICKS, tick, 0)
    cache_out = pltpu.make_async_copy(KV, kv_out.at[0], osem)
    cache_out.start()
    for k in range(NB):
        for c in range(CUTS):
            part = slice(c * width, (c + 1) * width)
            take(EX.at[TICKS, k, :, :, pl.ds(c * width, width)], exs.at[TICKS, k, c])
            total = EX[TICKS, k, 0, :, part].astype(jnp.float32) + EX[TICKS, k, 1, :, part].astype(jnp.float32)
            out_ref[0, pl.ds(k * PIECE, PIECE), part] = total.astype(jnp.bfloat16)
    take_pieces(NB, zs0)
    for t in range(TICKS):
        take_pieces(6 * NP, ss.at[t])
        take_pieces(2 * NP if t < TICKS - 1 else NP, zs.at[t])
    cache_out.wait()


def local(n_sections, x0, kv, wqkv, wout, gain, counts, order):
    entries, model = x0.shape[1:]
    tokens, inner = kv.shape[2:]
    NP = 2 * entries // PIECE
    NB = NP // 2
    rows = 8 * entries
    bf16, f32 = jnp.bfloat16, jnp.float32
    piece = (PIECE, model)
    dma = pltpu.SemaphoreType.DMA
    any_space = pl.BlockSpec(memory_space=pl.ANY)
    vmem = pl.BlockSpec(memory_space=pltpu.VMEM)
    smem = pl.BlockSpec(memory_space=pltpu.SMEM)
    return pl.pallas_call(
        functools.partial(relay_kernel, n_sections),
        out_shape=(
            jax.ShapeDtypeStruct((1, entries, model), bf16),
            jax.ShapeDtypeStruct((1, 2, tokens, inner), bf16),
        ),
        in_specs=[smem, smem, any_space, any_space, any_space, any_space, vmem],
        out_specs=(vmem, any_space),
        scratch_shapes=[
            pltpu.VMEM((TICKS * NP, 4) + piece, bf16),
            pltpu.VMEM((TICKS, NP, 4) + piece, bf16),
            pltpu.VMEM((TICKS, NP, 3) + piece, bf16),
            pltpu.VMEM((TICKS + 1, NP, 2) + piece, bf16),
            pltpu.VMEM((TICKS, NP) + piece, bf16),
            pltpu.VMEM((model, 3 * inner), bf16),
            pltpu.VMEM((inner, model), bf16),
            pltpu.VMEM((2, tokens, inner), bf16),
            pltpu.VMEM((rows, inner), bf16),
            pltpu.VMEM((rows, inner), bf16),
            pltpu.VMEM((rows, inner), bf16),
            pltpu.VMEM((rows, inner), f32),
            pltpu.VMEM((rows, inner), f32),
            dma((5,)), dma((NB,)), dma((TICKS,)), dma((TICKS,)), dma,
            dma((TICKS, NP, CUTS)), dma((TICKS + 1, NP, CUTS)), dma((TICKS, NP, 4)), dma,
        ],
        compiler_params=pltpu.CompilerParams(
            collective_id=0, has_side_effects=True, vmem_limit_bytes=56 * 1024 * 1024
        ),
    )(counts, order, x0, kv, jnp.transpose(wqkv, (0, 2, 1, 3)), wout, gain)


def solution(mesh):
    placed = (
        P("section", "sp", None),
        P("section", None, None, "sp"),
        P("section", None, None, "sp"),
        P("section", "sp", None),
        P("section", None),
        P(),
        P(),
    )
    return jax.shard_map(
        functools.partial(local, mesh.shape["section"]),
        mesh=mesh,
        in_specs=placed,
        out_specs=(P("section", "sp", None), P("section", None, None, "sp")),
        check_vma=False,
    )
```

```python
import functools
import math

import jax
import jax.numpy as jnp
from jax import lax
from jax.experimental import pallas as pl
from jax.experimental.pallas import tpu as pltpu
from jax.sharding import PartitionSpec as P

HD = 128
TICKS = 4
SCORE_GAIN = 2.5
EPSILON = 1e-06
PIECE = 16
SHIFT = 16.0
MESH = pl.DeviceIdType.MESH
CUTS = 2
HEAD = ("a0", "h1", "h2", "k3")
TAIL = ("c0", "q", "c1", "c2", "c3", "e0", "e1", "e2", "f0", "e3", "f1", "u", "f2", "b0", "f3")


def relay_kernel(
    n_sections, counts_ref, order_ref, x0_ref, kv_hbm, wqkv_hbm, wout_hbm, gain_ref, out_ref, kv_out,
    X, PA, RL, EX, S, W, WO, KV, Q, KF, VF, O, L, wsem, xsem, ss, zs, zs0, rls, exs, ags, osem,
):
    model = X.shape[-1]
    inner = KV.shape[-1]
    heads = inner // HD
    tokens = KV.shape[1]
    NP = PA.shape[1]
    NB = NP // 2
    rows = 4 * PIECE
    width = model // CUTS
    patches = order_ref.shape[0]

    section, sp = lax.axis_index("section"), lax.axis_index("sp")
    zh, y = sp // 4, sp % 4
    later, before = (section + 1) % n_sections, (section + n_sections - 1) % n_sections
    up, down = (section, zh * 4 + (y + 1) % 4), (section, zh * 4 + (y + 3) % 4)
    across = (section, (1 - zh) * 4 + y)
    opposite = (section, zh * 4 + (y + 2) % 4)
    next_same, next_other = (later, zh * 4 + y), (later, (1 - zh) * 4 + y)

    def send(src, dst, send_sem, recv_sem, device):
        pltpu.make_async_remote_copy(
            src_ref=src, dst_ref=dst, send_sem=send_sem, recv_sem=recv_sem, device_id=device, device_id_type=MESH
        ).start()

    def take(view, sem):
        pltpu.make_async_copy(view, view, sem).wait()

    def take_pieces(count, sem):
        take(X.at[pl.ds(0, count // 4)] if count % 4 == 0 else X.at[0, pl.ds(0, count)], sem)

    loads = [pltpu.make_async_copy(kv_hbm.at[0], KV, wsem.at[4])]
    for j in range(3):
        loads.append(pltpu.make_async_copy(wqkv_hbm.at[0, j], W.at[:, pl.ds(j * inner, inner)], wsem.at[j]))
    loads.append(pltpu.make_async_copy(wout_hbm.at[0], WO, wsem.at[3]))
    starts = [
        pltpu.make_async_copy(x0_ref.at[0, pl.ds(k * PIECE, PIECE)], X.at[zh * NB + k, 0], xsem.at[k]) for k in range(NB)
    ]
    for copy in starts + loads:
        copy.start()

    barrier = pltpu.get_barrier_semaphore()
    friends = [up, down, opposite, across, next_same, next_other, (before, zh * 4 + y), (before, (1 - zh) * 4 + y)]
    for device in friends:
        pl.semaphore_signal(barrier, inc=1, device_id=device, device_id_type=MESH)
    pl.semaphore_wait(barrier, len(friends))

    for copy in starts:
        copy.wait()
    for k in range(NB):
        for c in range(CUTS):
            piece = X.at[zh * NB + k, 0, :, pl.ds(c * width, width)]
            send(piece, piece, zs0, exs.at[0, zh * NB + k, c], across)
    local = lax.broadcasted_iota(jnp.int32, (1, NP * rows), 1)
    slot = (local % rows) // PIECE
    chunk = (y + jnp.where(slot == 1, 1, jnp.where(slot == 2, 3, jnp.where(slot == 3, 2, 0)))) % 4
    within = (local // rows) * PIECE + local % PIECE
    global_row = (within // 32) * 128 + chunk * 32 + within % 32
    token = lax.broadcasted_iota(jnp.int32, (1, tokens), 1)
    gain = gain_ref[...]
    factor = SCORE_GAIN / math.sqrt(HD) * math.log2(math.e)
    shift = SHIFT * math.log2(math.e)

    def gather(t, at, i, c):
        spot = pl.ds(c * width, width)
        for k, device in ((3, opposite), (2, up), (1, down)):
            send(X.at[at, 0, :, spot], X.at[at, k, :, spot], ss.at[t], ags.at[t, i, k], device)

    for i in range(NP):
        ii = (i + zh * NB) % NP
        for c in range(CUTS):
            if i >= NB:
                take(X.at[ii, 0, :, pl.ds(c * width, width)], exs.at[0, ii, c])
            gather(0, ii, ii, c)
    for copy in loads:
        copy.wait()

    def head_norm(part):
        spread = jnp.mean(part * part, axis=-1, keepdims=True)
        return (part * lax.rsqrt(spread + EPSILON)).astype(jnp.bfloat16)

    def scores(query, keys, bias):
        s = lax.dot_general(query, keys, (((1,), (1,)), ((), ())), preferred_element_type=jnp.float32)
        return jnp.exp2(s * factor + bias)

    def plan(t):
        patch = order_ref[(section + TICKS * n_sections - t) % patches]
        length, first = jnp.int32(0), jnp.int32(0)
        for r in range(patches):
            length = length + jnp.where(patch == r, counts_ref[r], 0)
            first = first + jnp.where(r < patch, counts_ref[r], 0)
        held_bias = jnp.where((token >= first) & (token < first + length), -1e30, -shift)
        return length, first, held_bias

    def tick(t, _):
        length, first, held_now = plan(t)
        fresh_bias = jnp.where(global_row < length, -shift, -1e30)

        def stage_f(i):
            @pl.when(t < TICKS - 1)
            def _():
                at = (t + 1) * NP + i
                for c in range(CUTS):
                    part = slice(c * width, (c + 1) * width)
                    take(EX.at[t + 1, i, :, :, pl.ds(c * width, width)], exs.at[t + 1, i, c])
                    total = EX[t + 1, i, 0, :, part].astype(jnp.float32) + EX[t + 1, i, 1, :, part].astype(jnp.float32)
                    X[at, 0, :, part] = total.astype(jnp.bfloat16)
                    gather(t + 1, at, i, c)

        def stage_h(i, whole=True, t=t, held_bias=held_now):
            ii = (i + jnp.where(t == 0, zh * NB, 0)) % NP
            at = t * NP + ii
            for k in (1, 2, 3):
                take(X.at[at, k], ags.at[t, ii, k])
            x = X[at].reshape(rows, model).astype(jnp.float32)
            spread = jnp.mean(x * x, axis=-1, keepdims=True)
            normed = (x * lax.rsqrt(spread + EPSILON) * gain).astype(jnp.bfloat16)
            here = pl.ds(pl.multiple_of(ii * rows, rows), rows)

            pairs = jnp.dot(normed, W[:, inner:], preferred_element_type=jnp.float32)
            keys = pairs[:, :inner]
            VF[here, :] = pairs[:, inner:].astype(jnp.bfloat16)
            for h in range(heads):
                cols = slice(h * HD, (h + 1) * HD)
                KF[here, cols] = head_norm(keys[:, cols])

            def finish():
                queries = jnp.dot(normed, W[:, :inner], preferred_element_type=jnp.float32)
                for h in range(heads):
                    cols = slice(h * HD, (h + 1) * HD)
                    query = head_norm(queries[:, cols])
                    Q[here, cols] = query
                    e = scores(query, KV[0, :, cols], held_bias)
                    L[here, cols] = jnp.broadcast_to(jnp.sum(e, axis=-1, keepdims=True), (rows, HD))
                    O[here, cols] = jnp.dot(e.astype(jnp.bfloat16), KV[1, :, cols], preferred_element_type=jnp.float32)

            if whole:
                finish()
            return finish

        def stage_c(i):
            here = slice(i * rows, (i + 1) * rows)
            attended = []
            for h in range(heads):
                cols = slice(h * HD, (h + 1) * HD)
                e = scores(Q[here, cols], KF[:, cols], fresh_bias)
                total = L[here, cols] + jnp.sum(e, axis=-1, keepdims=True)
                mixed = O[here, cols] + jnp.dot(
                    e.astype(jnp.bfloat16), VF[:, cols], preferred_element_type=jnp.float32
                )
                attended.append((mixed / total).astype(jnp.bfloat16))
            attended = jnp.concatenate(attended, axis=1)
            for c in range(CUTS):
                part = slice(c * width, (c + 1) * width)
                spot = pl.ds(c * width, width)
                partial = jnp.dot(attended, WO[:, part], preferred_element_type=jnp.float32)
                PA[t, i, :, :, part] = partial.astype(jnp.bfloat16).reshape(4, PIECE, width)
                for k, device in ((3, opposite), (1, up), (2, down)):
                    send(PA.at[t, i, k, :, spot], RL.at[t, i, k - 1, :, spot], ss.at[t], rls.at[t, i, c], device)

        def stage_e(i):
            for c in range(CUTS):
                part = slice(c * width, (c + 1) * width)
                spot = pl.ds(c * width, width)
                take(RL.at[t, i, :, :, spot], rls.at[t, i, c])
                total = PA[t, i, 0, :, part].astype(jnp.float32)
                for k in range(3):
                    total = total + RL[t, i, k, :, part].astype(jnp.float32)
                total = total + jnp.where(zh == i // NB, X[t * NP + i, 0, :, part].astype(jnp.float32), 0.0)
                S[t, i, :, part] = total.astype(jnp.bfloat16)
                mine = S.at[t, i, :, spot]

                @pl.when(t < TICKS - 1)
                def _():
                    send(mine, EX.at[t + 1, i, 1, :, spot], zs.at[t], exs.at[t + 1, i, c], next_other)
                    send(mine, EX.at[t + 1, i, 0, :, spot], zs.at[t], exs.at[t + 1, i, c], next_same)

                @pl.when(t == TICKS - 1)
                def _():
                    k = i % NB
                    target = (later, (i // NB) * 4 + y)
                    send(mine, EX.at[TICKS, k, zh, :, spot], zs.at[t], exs.at[TICKS, k, c], target)

        def update():
            for b in range(3):
                span = tokens // 3
                at = pl.ds(b * span, span)
                row = lax.broadcasted_iota(jnp.int32, (span, 1), 0) + (b * span - first)
                hit = (row == global_row) & (global_row < length)
                pick = jnp.where(hit, 1.0, 0.0).astype(jnp.bfloat16)
                inside = (row >= 0) & (row < length)
                for part, fresh in ((0, KF), (1, VF)):
                    moved = jnp.dot(pick, fresh[...], preferred_element_type=jnp.float32)
                    kept = KV[part, at, :].astype(jnp.float32)
                    KV[part, at, :] = jnp.where(inside, moved, kept).astype(jnp.bfloat16)

        def stage_a(i):
            @pl.when(t == 0)
            def _():
                stage_h(i)

        def stage_b(i):
            @pl.when(t < TICKS - 1)
            def _():
                stage_h(i, True, t + 1, plan(t + 1)[2])

        stages = dict(a=stage_a, b=stage_b, h=stage_h, c=stage_c, e=stage_e, f=stage_f)
        finish = None
        for step in HEAD + TAIL:
            kind, i = step[0], int(step[1:] or 0)
            if kind == "k":
                finish = stage_h(i, False)
            elif kind == "q":
                finish()
            elif kind == "u":
                update()
            else:
                stages[kind](i)
        return 0

    lax.fori_loop(0, TICKS, tick, 0)
    cache_out = pltpu.make_async_copy(KV, kv_out.at[0], osem)
    cache_out.start()
    for k in range(NB):
        for c in range(CUTS):
            part = slice(c * width, (c + 1) * width)
            take(EX.at[TICKS, k, :, :, pl.ds(c * width, width)], exs.at[TICKS, k, c])
            total = EX[TICKS, k, 0, :, part].astype(jnp.float32) + EX[TICKS, k, 1, :, part].astype(jnp.float32)
            out_ref[0, pl.ds(k * PIECE, PIECE), part] = total.astype(jnp.bfloat16)
    take_pieces(NB, zs0)
    for t in range(TICKS):
        take_pieces(6 * NP, ss.at[t])
        take_pieces(2 * NP if t < TICKS - 1 else NP, zs.at[t])
    cache_out.wait()


def local(n_sections, x0, kv, wqkv, wout, gain, counts, order):
    entries, model = x0.shape[1:]
    tokens, inner = kv.shape[2:]
    NP = 2 * entries // PIECE
    NB = NP // 2
    rows = 8 * entries
    bf16, f32 = jnp.bfloat16, jnp.float32
    piece = (PIECE, model)
    dma = pltpu.SemaphoreType.DMA
    any_space = pl.BlockSpec(memory_space=pl.ANY)
    vmem = pl.BlockSpec(memory_space=pltpu.VMEM)
    smem = pl.BlockSpec(memory_space=pltpu.SMEM)
    return pl.pallas_call(
        functools.partial(relay_kernel, n_sections),
        out_shape=(
            jax.ShapeDtypeStruct((1, entries, model), bf16),
            jax.ShapeDtypeStruct((1, 2, tokens, inner), bf16),
        ),
        in_specs=[smem, smem, any_space, any_space, any_space, any_space, vmem],
        out_specs=(vmem, any_space),
        scratch_shapes=[
            pltpu.VMEM((TICKS * NP, 4) + piece, bf16),
            pltpu.VMEM((TICKS, NP, 4) + piece, bf16),
            pltpu.VMEM((TICKS, NP, 3) + piece, bf16),
            pltpu.VMEM((TICKS + 1, NP, 2) + piece, bf16),
            pltpu.VMEM((TICKS, NP) + piece, bf16),
            pltpu.VMEM((model, 3 * inner), bf16),
            pltpu.VMEM((inner, model), bf16),
            pltpu.VMEM((2, tokens, inner), bf16),
            pltpu.VMEM((rows, inner), bf16),
            pltpu.VMEM((rows, inner), bf16),
            pltpu.VMEM((rows, inner), bf16),
            pltpu.VMEM((rows, inner), f32),
            pltpu.VMEM((rows, inner), f32),
            dma((5,)), dma((NB,)), dma((TICKS,)), dma((TICKS,)), dma,
            dma((TICKS, NP, CUTS)), dma((TICKS + 1, NP, CUTS)), dma((TICKS, NP, 4)), dma,
        ],
        compiler_params=pltpu.CompilerParams(
            collective_id=0, has_side_effects=True, vmem_limit_bytes=56 * 1024 * 1024
        ),
    )(counts, order, x0, kv, jnp.transpose(wqkv, (0, 2, 1, 3)), wout, gain)


def solution(mesh):
    placed = (
        P("section", "sp", None),
        P("section", None, None, "sp"),
        P("section", None, None, "sp"),
        P("section", "sp", None),
        P("section", None),
        P(),
        P(),
    )
    return jax.shard_map(
        functools.partial(local, mesh.shape["section"]),
        mesh=mesh,
        in_specs=placed,
        out_specs=(P("section", "sp", None), P("section", None, None, "sp")),
        check_vma=False,
    )
```
